32 devices in a mesh: frow: 8 (over z, y), fcol: 4 (over x, core).
Axes of the slice: x: 2, y: 2, z: 4, core: 2. Of those that a mesh axis runs over, the one named last changes fastest.
Arguments:
- front_orig: float32 [8, 2048, 4, 4096], P('frow', None, 'fcol'), may hold values from -0.1 to 45, as said below
- child_tiles: bfloat16 [2048, 128, 128], P(('frow', 'fcol')), may hold values from -0.25 to 0.25
- tile_target: int32 [2048, 2], P(('frow', 'fcol')), may hold values from 0 to 511, as said below
- tile_rows: int32 [2048, 128], P(('frow', 'fcol')), may hold values from 0 to 127, each once within a row
- tile_cols: int32 [2048, 128], P(('frow', 'fcol')), may hold values from 0 to 127, each once within a row
Outputs:
- front_out: float32 [8, 2048, 4, 4096], P('frow', None, 'fcol')
The draws below stay inside these ranges and needn't reach their ends.
Inputs may be any that keep to these rules, and one draw needn't show every extreme that they name: `front_orig`: Symmetric; the lower triangle of the front after every tile is added defines a positive definite matrix. `tile_target`: rows come 64 to a device in device order. Column 0 is the owner, frow index times 4 plus fcol index; column 1 the local block on that owner, local block row times 32 plus local block column; the block lies on or below the front's block diagonal. At most 2 tiles of one device go to one owner, and one owner receives exactly 2 from every device.
All inputs are finite; a program needn't handle non-finite values.
Results may differ from the reference program's by a relative error of at most 0.0003.
Values may be sent and summed in bfloat16 or wider, within the bound.
A program may use at most 192 MiB of HBM per device.

```python
import math
import jax
import jax.numpy as jnp
from jax import lax

F = 16384
NB = 128
PW = 512
NPANEL = 2
TPD = 64
CAP = 2
ROWGRID = 8
COLGRID = 4
OWNERS = 32
LRB = 16
LCB = 32
TILES = 2048


def to_grid_drawn(natural):
    shaped = natural.reshape(LRB, ROWGRID, NB, LCB, COLGRID, NB)
    return shaped.transpose(1, 0, 2, 4, 3, 5).reshape(ROWGRID, LRB * NB, COLGRID, LCB * NB)


def draw_front_orig(key, part):
    noise_key, diag_key, scale_key = jax.random.split(jax.random.fold_in(key, 11), 3)
    noise_part = jnp.clip(0.01 * jax.random.normal(noise_key, (F, F), jnp.float32), -0.05, 0.05)
    scales = jnp.exp(jax.random.uniform(scale_key, (F,), jnp.float32, -0.35, 0.35))
    amplitude = 0.8
    grid_rows = F // NB
    row_ids = jnp.arange(grid_rows, dtype=jnp.float32)
    col_ids = jnp.arange(NB, dtype=jnp.float32)
    row_length = ROWGRID * 0.5
    col_length = NB * 0.125
    row_kernel = jnp.exp(-jnp.abs(row_ids[:, None] - row_ids[None, :]) / row_length)
    col_kernel = jnp.exp(-jnp.abs(col_ids[:, None] - col_ids[None, :]) / col_length)
    kernel = (row_kernel[:, None, :, None] * col_kernel[None, :, None, :]).reshape(F, F)
    coupled = amplitude * scales[:, None] * scales[None, :] * kernel
    symmetric = 0.5 * (noise_part + noise_part.T)
    diagonal = jnp.exp(jax.random.uniform(diag_key, (F,), jnp.float32, math.log(20.0), math.log(40.0)))
    on_diagonal = jnp.arange(F)[:, None] == jnp.arange(F)[None, :]
    full = coupled + jnp.where(on_diagonal, diagonal[None, :], symmetric)
    return to_grid_drawn(full).astype(jnp.float32)


def draw_child_tiles(key, part):
    tile_key = jax.random.fold_in(key, 23)
    values = jnp.clip(0.025 * jax.random.normal(tile_key, (TILES, NB, NB), jnp.float32), -0.15, 0.15)
    return values.astype(jnp.bfloat16)


def draw_tile_target(key, part):
    keys = jax.random.split(jax.random.fold_in(key, 37), 6)
    position_merit_aggregate = OWNERS * CAP
    random_perturbation = jax.random.randint(keys[0], (OWNERS, position_merit_aggregate), 0, 65536)
    pull_strength = jax.random.randint(keys[1], (OWNERS,), 0, 65536)
    favored_position_choice = jax.random.randint(keys[2], (), 0, OWNERS)
    position_numbers = jnp.arange(position_merit_aggregate, dtype=jnp.int32)
    position_occupant = position_numbers // CAP
    closeness_reward = jnp.where(position_occupant == favored_position_choice, 131072, 0)
    position_merits = (random_perturbation + jnp.take(pull_strength, position_occupant)[None, :] + closeness_reward[None, :]) * position_merit_aggregate + position_numbers[None, :]
    chosen = jax.lax.top_k(position_merits, TPD)[1]
    shuffle_keys = jax.random.split(keys[3], OWNERS)
    shuffles = jax.vmap(lambda sub_key: jax.random.permutation(sub_key, TPD))(shuffle_keys)
    chosen = jnp.take_along_axis(chosen, shuffles, axis=1)
    owner_of = (chosen // CAP).astype(jnp.int32)
    prow = owner_of // COLGRID
    pcol = owner_of % COLGRID
    col_most = jnp.minimum(LCB - 1, ((LRB - 1) * ROWGRID + prow - pcol) // COLGRID)
    col_pick = jax.random.randint(keys[4], owner_of.shape, 0, col_most + 1)
    row_least = jnp.maximum(0, -((prow - pcol - col_pick * COLGRID) // ROWGRID))
    row_pick = jax.random.randint(keys[5], owner_of.shape, row_least, LRB)
    block_of = row_pick * LCB + col_pick
    return jnp.stack([owner_of.reshape(-1), block_of.reshape(-1)], axis=1).astype(jnp.int32)


def setup_inputs(seed: int = 0) -> dict:
    splits = jax.random.split(jax.random.key(seed), 6)
    return {
        "front_orig": draw_front_orig(jax.random.fold_in(splits[5], 71), 0),
        "child_tiles": draw_child_tiles(jax.random.fold_in(splits[5], 71), 0),
        "tile_target": draw_tile_target(jax.random.fold_in(splits[5], 71), 0),
        "tile_rows": jax.vmap(lambda own: jax.random.permutation(own, NB))(jax.random.split(splits[3], TILES)).reshape((TILES, NB)).astype(jnp.int32),
        "tile_cols": jax.vmap(lambda own: jax.random.permutation(own, NB))(jax.random.split(splits[4], TILES)).reshape((TILES, NB)).astype(jnp.int32),
    }


def to_natural(grid_matrix):
    shaped = grid_matrix.reshape(ROWGRID, LRB, NB, COLGRID, LCB, NB)
    return shaped.transpose(1, 0, 2, 4, 3, 5).reshape(F, F)

def to_grid(natural):
    shaped = natural.reshape(LRB, ROWGRID, NB, LCB, COLGRID, NB)
    return shaped.transpose(1, 0, 2, 4, 3, 5).reshape(ROWGRID, LRB * NB, COLGRID, LCB * NB)

def reference(front_orig, child_tiles, tile_target, tile_rows, tile_cols):
    owner_of = tile_target[:, 0].astype(jnp.int32)
    block_of = tile_target[:, 1].astype(jnp.int32)
    block_row = block_of // LCB * ROWGRID + owner_of // COLGRID
    block_col = block_of % LCB * COLGRID + owner_of % COLGRID
    row_pos = (block_row[:, None] * NB + tile_rows).astype(jnp.int32)
    col_pos = (block_col[:, None] * NB + tile_cols).astype(jnp.int32)
    flat_pos = (row_pos[:, :, None] * F + col_pos[:, None, :]).reshape(-1).astype(jnp.int32)
    values = child_tiles.astype(jnp.float32).reshape(-1)
    matrix = to_natural(front_orig).reshape(-1).at[flat_pos].add(values).reshape(F, F)
    for panel_idx in range(NPANEL):
        start = panel_idx * PW
        stop = start + PW
        diag_block = matrix[start:stop, start:stop]
        symmetric = jnp.tril(diag_block) + jnp.tril(diag_block, -1).T
        factor = jnp.linalg.cholesky(symmetric)
        below = matrix[stop:, start:stop]
        solved = lax.linalg.triangular_solve(factor, below, left_side=False, lower=True, transpose_a=True)
        update = jnp.dot(solved.astype(jnp.float32), solved.T.astype(jnp.float32), precision=lax.Precision.HIGHEST, preferred_element_type=jnp.float32)
        matrix = matrix.at[stop:, stop:].add(-update)
        matrix = matrix.at[start:stop, start:stop].set(factor)
        matrix = matrix.at[stop:, start:stop].set(solved)
    return to_grid(jnp.tril(matrix))
```

```python
import functools

import jax
import jax.numpy as jnp
from jax import lax
from jax.experimental import pallas as pl
from jax.experimental.pallas import tpu as pltpu
from jax.sharding import PartitionSpec as P

PW = 512
NPANEL = 2
CAP = 2
NB = 128
GROUP = 8
WIDE = PW * NPANEL
BLOCKS = WIDE // NB
HIGHEST = lax.Precision.HIGHEST


def dot_tn(a, b):
    return lax.dot_general(
        a, b, (((0,), (0,)), ((), ())), precision=HIGHEST, preferred_element_type=jnp.float32
    )


def factor_block(t_ref):
    lane = lax.broadcasted_iota(jnp.int32, (GROUP, NB), 1)
    sub = lax.broadcasted_iota(jnp.int32, (GROUP, NB), 0)
    for first in range(0, NB, GROUP):
        rows = t_ref[first : first + GROUP, :]
        w = [rows[k : k + 1, :] for k in range(GROUP)]
        s = {}
        for a in range(GROUP):
            for b in range(a, GROUP):
                s[a, b] = jnp.broadcast_to(rows[a : a + 1, first + b : first + b + 1], (1, NB))
        for k in range(GROUP):
            scale = lax.rsqrt(s[k, k])
            scale2 = jnp.concatenate([scale, scale], axis=1)
            w[k] = w[k] * scale2
            coef = {m: s[k, m] * scale for m in range(k + 1, GROUP)}
            for m in range(k + 1, GROUP):
                for n in range(m, GROUP):
                    s[m, n] = s[m, n] - coef[m] * coef[n]
                w[m] = w[m] - jnp.concatenate([coef[m], coef[m]], axis=1) * w[k]
        done = jnp.concatenate(w, axis=0)
        upper = jnp.where(lane >= first + sub, done[:, :NB], 0.0)
        done = jnp.concatenate([upper, done[:, NB:]], axis=1)
        t_ref[first : first + GROUP, :] = done
        if first + GROUP < NB:
            change = dot_tn(upper, done)
            t_ref[first + GROUP :, :] -= change[first + GROUP :, :]


def factor_kernel(d_ref, m_ref, u_ref, t_ref, p_ref):
    m_ref[...] = d_ref[...]
    r = lax.broadcasted_iota(jnp.int32, (NB, NB), 0)
    c = lax.broadcasted_iota(jnp.int32, (NB, NB), 1)

    def step(k, _):
        here = pl.ds(pl.multiple_of(k * NB, NB), NB)
        t_ref[:, :NB] = m_ref[here, here]
        t_ref[:, NB:] = jnp.where(r == c, 1.0, 0.0)
        factor_block(t_ref)
        u_ref[here, :] = t_ref[:, :NB]
        inverse = t_ref[:, NB:]
        p_ref[...] = jnp.dot(
            inverse, m_ref[here, :], precision=HIGHEST, preferred_element_type=jnp.float32
        )
        p_ref[:, here] = inverse
        m_ref[here, :] = p_ref[...]

        def below(i, _):
            there = pl.ds(pl.multiple_of(i * NB, NB), NB)
            m_ref[there, here] = jnp.zeros((NB, NB), jnp.float32)
            m_ref[there, :] -= dot_tn(p_ref[:, there], p_ref[...])
            return 0

        lax.fori_loop(k + 1, BLOCKS, below, 0)
        return 0

    lax.fori_loop(0, BLOCKS, step, 0)


def factor_diagonal(diag):
    return pl.pallas_call(
        factor_kernel,
        out_shape=(
            jax.ShapeDtypeStruct((WIDE, WIDE), jnp.float32),
            jax.ShapeDtypeStruct((WIDE, NB), jnp.float32),
        ),
        in_specs=[pl.BlockSpec(memory_space=pltpu.VMEM)],
        out_specs=(
            pl.BlockSpec(memory_space=pltpu.VMEM),
            pl.BlockSpec(memory_space=pltpu.VMEM),
        ),
        scratch_shapes=[
            pltpu.VMEM((NB, 2 * NB), jnp.float32),
            pltpu.VMEM((NB, WIDE), jnp.float32),
        ],
        compiler_params=pltpu.CompilerParams(vmem_limit_bytes=32 * 1024 * 1024),
        cost_estimate=pl.CostEstimate(
            flops=20 * WIDE**3, bytes_accessed=WIDE * WIDE * 8, transcendentals=WIDE
        ),
    )(diag)


STEP = 2
CHUNK = 4


def update_kernel(
    row_devs, col_devs, nc, own, ids, pos, front_ref, rowf_ref, colf_ref, panel_ref, tiles_ref, out_ref
):
    g = pl.program_id(0)
    row_here, col_here = pos[0], pos[1]
    r = lax.broadcasted_iota(jnp.int32, (NB, NB), 0)
    c = lax.broadcasted_iota(jnp.int32, (NB, NB), 1)

    def place(b, col):
        return pl.ds(b * NB * nc + col, NB, stride=nc)

    last_row = (g * STEP + STEP - 1) * row_devs + row_here
    for chunk in range(0, nc, CHUNK):
        active = chunk * col_devs + col_here <= last_row

        @pl.when(active)
        def _(chunk=chunk):
            product = lax.dot_general(
                rowf_ref[...],
                colf_ref[chunk * NB : (chunk + CHUNK) * NB, :],
                (((1,), (1,)), ((), ())),
                preferred_element_type=jnp.float32,
            )
            for b in range(STEP):
                row_block = (g * STEP + b) * row_devs + row_here
                for cc in range(CHUNK):
                    col = chunk + cc
                    if col < own:
                        out_ref[place(b, col), :] = panel_ref[
                            b * NB : (b + 1) * NB, col * NB : (col + 1) * NB
                        ]
                    else:
                        gap = (row_block - (col * col_devs + col_here)) * NB
                        value = (
                            front_ref[place(b, col), :]
                            - product[b * NB : (b + 1) * NB, cc * NB : (cc + 1) * NB]
                        )
                        out_ref[place(b, col), :] = jnp.where(r + gap >= c, value, 0.0)

        @pl.when(jnp.logical_not(active))
        def _(chunk=chunk):
            for b in range(STEP):
                for cc in range(CHUNK):
                    out_ref[place(b, chunk + cc), :] = jnp.zeros((NB, NB), jnp.float32)

    def add_tile(t, _):
        block = ids[t]
        br = block // nc
        bc = block % nc

        @pl.when((br // STEP == g) & (bc >= own))
        def _():
            gap = (br * row_devs + row_here - (bc * col_devs + col_here)) * NB
            tile = tiles_ref[t].astype(jnp.float32)
            where = place(br % STEP, bc)
            out_ref[where, :] += jnp.where(r + gap >= c, tile, 0.0)

        return 0

    lax.fori_loop(0, tiles_ref.shape[0], add_tile, 0)


def update(front, rowf, colf, panel, tiles, ids, pos, row_devs, col_devs):
    rows, cols = rowf.shape[0], colf.shape[0]
    nc = cols // NB
    own = panel.shape[1] // NB
    height = STEP * NB
    return pl.pallas_call(
        functools.partial(update_kernel, row_devs, col_devs, nc, own),
        out_shape=jax.ShapeDtypeStruct((rows * nc, NB), jnp.float32),
        grid_spec=pltpu.PrefetchScalarGridSpec(
            num_scalar_prefetch=2,
            grid=(rows // height,),
            in_specs=[
                pl.BlockSpec((height * nc, NB), lambda g, *_: (g, 0)),
                pl.BlockSpec((height, WIDE), lambda g, *_: (g, 0)),
                pl.BlockSpec(memory_space=pltpu.VMEM),
                pl.BlockSpec((height, own * NB), lambda g, *_: (g, 0)),
                pl.BlockSpec(memory_space=pltpu.VMEM),
            ],
            out_specs=pl.BlockSpec((height * nc, NB), lambda g, *_: (g, 0)),
        ),
        compiler_params=pltpu.CompilerParams(vmem_limit_bytes=48 * 1024 * 1024),
        cost_estimate=pl.CostEstimate(
            flops=rows * cols * WIDE, bytes_accessed=rows * cols * 8, transcendentals=0
        ),
    )(ids, pos, front, rowf, colf, panel, tiles)


def place_tiles(tile_block, perm_block):
    width = tile_block.shape[-1]
    positions = jnp.arange(width, dtype=jnp.int32)
    row_onehot = (perm_block[:, 0, None, :] == positions[:, None]).astype(jnp.bfloat16)
    col_onehot = (perm_block[:, 1, None, :] == positions[:, None]).astype(jnp.bfloat16)
    moved = jnp.einsum(
        "axi,aij->axj", row_onehot, tile_block, preferred_element_type=jnp.float32
    ).astype(jnp.bfloat16)
    return jnp.einsum(
        "axj,ayj->axy", moved, col_onehot, preferred_element_type=jnp.float32
    ).astype(jnp.bfloat16)


def exchange(x):
    return lax.all_to_all(x, ("frow", "fcol"), split_axis=0, concat_axis=0, tiled=True)


def shards(front_orig, child_tiles, tile_target, tile_rows, tile_cols):
    row_devs = lax.axis_size("frow")
    col_devs = lax.axis_size("fcol")
    owners = row_devs * col_devs
    row_here = lax.axis_index("frow")
    col_here = lax.axis_index("fcol")
    held = child_tiles.shape[0]
    slot_count = owners * CAP
    owner_of = tile_target[:, 0]
    block_of = tile_target[:, 1]
    tile_order = jnp.arange(held, dtype=jnp.int32)
    same_owner = owner_of[:, None] == owner_of[None, :]
    earlier = tile_order[None, :] < tile_order[:, None]
    rank_of = jnp.sum(jnp.where(same_owner & earlier, 1, 0), axis=1).astype(jnp.int32)
    slot_of = owner_of * CAP + rank_of
    slot_match = slot_of[None, :] == jnp.arange(slot_count, dtype=jnp.int32)[:, None]
    source_tile = jnp.sum(jnp.where(slot_match, tile_order[None, :], 0), axis=1)
    lists = jnp.stack(
        [tile_rows, tile_cols, jnp.broadcast_to(block_of[:, None], tile_rows.shape)], axis=1
    )
    lists_in = exchange(jnp.take(lists, source_tile, axis=0).reshape(owners, CAP, 3, NB))
    tiles_in = exchange(jnp.take(child_tiles, source_tile, axis=0).reshape(owners, CAP, NB, NB))
    lists_in = lists_in.reshape(slot_count, 3, NB)
    ids = lists_in[:, 2, 0]
    placed = place_tiles(tiles_in.reshape(slot_count, NB, NB), lists_in[:, :2])

    rows, cols = front_orig.shape[1], front_orig.shape[3]
    lrb, nc = rows // NB, cols // NB
    own = BLOCKS // col_devs
    ratio = row_devs // col_devs

    panel_ids = (jnp.arange(lrb)[:, None] * nc + jnp.arange(own)[None, :]).reshape(-1, 1)
    panel_onehot = (ids[None, :] == panel_ids).astype(jnp.bfloat16)
    added = jnp.dot(
        panel_onehot, placed.reshape(slot_count, NB * NB), preferred_element_type=jnp.float32
    )
    added = added.reshape(lrb, own, NB, NB).transpose(0, 2, 1, 3).reshape(rows, own * NB)
    own_panel = (front_orig[0, :, 0, : own * NB] + added).astype(jnp.bfloat16)

    corner = lax.all_gather(own_panel[:NB], ("frow", "fcol"), axis=0, tiled=False)
    corner = corner.reshape(row_devs, col_devs, NB, own, NB)[:BLOCKS]
    diag = corner.transpose(0, 2, 3, 1, 4).reshape(WIDE, WIDE).astype(jnp.float32)
    diag = jnp.tril(diag) + jnp.tril(diag, -1).T

    route = []
    for p in range(row_devs):
        for q in range(col_devs):
            route.append((p * col_devs + q, (q * ratio + p // col_devs) * col_devs + p % col_devs))
    turned = lax.ppermute(own_panel, ("frow", "fcol"), route)
    col_raw = lax.all_gather(turned, "frow", axis=0, tiled=False)
    col_raw = col_raw.reshape(col_devs, ratio, lrb, NB, own, NB)
    col_raw = col_raw.transpose(2, 1, 3, 4, 0, 5).reshape(cols, WIDE)
    row_raw = lax.all_gather(own_panel, "fcol", axis=0, tiled=False)
    row_raw = row_raw.reshape(col_devs, rows, own, NB).transpose(1, 2, 0, 3).reshape(rows, WIDE)

    packed, diag_upper = factor_diagonal(diag)
    inverse = jnp.tril(packed).astype(jnp.bfloat16)

    def solve(raw, dtype):
        return lax.dot_general(
            raw, inverse, (((1,), (1,)), ((), ())), preferred_element_type=jnp.float32
        ).astype(dtype)

    rowf = solve(row_raw, jnp.bfloat16)
    colf = solve(col_raw, jnp.bfloat16)
    own_inverse = lax.dynamic_index_in_dim(
        inverse.reshape(own, col_devs, NB, WIDE), col_here, axis=1, keepdims=False
    ).reshape(own * NB, WIDE)
    solved = lax.dot_general(
        row_raw, own_inverse, (((1,), (1,)), ((), ())), preferred_element_type=jnp.float32
    )
    block = jnp.minimum(row_here, BLOCKS - 1)
    above = lax.dynamic_slice(packed, (0, block * NB), (WIDE, NB))
    on = lax.dynamic_slice(diag_upper, (block * NB, 0), (NB, NB)).T
    corner_blocks = []
    for j in range(own):
        col_block = col_here + j * col_devs
        left = lax.dynamic_slice(above, (col_block * NB, 0), (NB, NB)).T
        corner_blocks.append(
            jnp.where(col_block < block, left, jnp.where(col_block == block, on, 0.0))
        )
    corner_own = jnp.where(
        row_here < BLOCKS, jnp.concatenate(corner_blocks, axis=1), solved[:NB]
    )
    panel = jnp.concatenate([corner_own, solved[NB:]], axis=0)

    out = update(
        front_orig.reshape(rows * nc, NB),
        rowf,
        colf,
        panel,
        placed,
        ids,
        jnp.stack([row_here, col_here]).astype(jnp.int32),
        row_devs,
        col_devs,
    )
    return out.reshape(front_orig.shape)


def solution(mesh):
    return jax.shard_map(
        shards,
        mesh=mesh,
        in_specs=(
            P("frow", None, "fcol", None),
            P(("frow", "fcol"), None, None),
            P(("frow", "fcol"), None),
            P(("frow", "fcol"), None),
            P(("frow", "fcol"), None),
        ),
        out_specs=P("frow", None, "fcol", None),
        check_vma=False,
    )
```

```python
import functools

import jax
import jax.numpy as jnp
from jax import lax
from jax.experimental import pallas as pl
from jax.experimental.pallas import tpu as pltpu
from jax.sharding import PartitionSpec as P

PW = 512
NPANEL = 2
CAP = 2
NB = 128
GROUP = 8
WIDE = PW * NPANEL
BLOCKS = WIDE // NB
HIGHEST = lax.Precision.HIGHEST


def dot_tn(a, b):
    return lax.dot_general(
        a, b, (((0,), (0,)), ((), ())), precision=HIGHEST, preferred_element_type=jnp.float32
    )


def factor_block(t_ref):
    lane = lax.broadcasted_iota(jnp.int32, (GROUP, NB), 1)
    sub = lax.broadcasted_iota(jnp.int32, (GROUP, NB), 0)
    for first in range(0, NB, GROUP):
        rows = t_ref[first : first + GROUP, :]
        w = [rows[k : k + 1, :] for k in range(GROUP)]
        s = {}
        for a in range(GROUP):
            for b in range(a, GROUP):
                s[a, b] = jnp.broadcast_to(rows[a : a + 1, first + b : first + b + 1], (1, NB))
        for k in range(GROUP):
            scale = lax.rsqrt(s[k, k])
            scale2 = jnp.concatenate([scale, scale], axis=1)
            w[k] = w[k] * scale2
            coef = {m: s[k, m] * scale for m in range(k + 1, GROUP)}
            for m in range(k + 1, GROUP):
                for n in range(m, GROUP):
                    s[m, n] = s[m, n] - coef[m] * coef[n]
                w[m] = w[m] - jnp.concatenate([coef[m], coef[m]], axis=1) * w[k]
        done = jnp.concatenate(w, axis=0)
        upper = jnp.where(lane >= first + sub, done[:, :NB], 0.0)
        done = jnp.concatenate([upper, done[:, NB:]], axis=1)
        t_ref[first : first + GROUP, :] = done
        if first + GROUP < NB:
            change = dot_tn(upper, done)
            t_ref[first + GROUP :, :] -= change[first + GROUP :, :]


def factor_kernel(row_devs, col_devs, d_ref, l_ref, inv_ref, m_ref, t_ref, p_ref):
    r = lax.broadcasted_iota(jnp.int32, (NB, NB), 0)
    c = lax.broadcasted_iota(jnp.int32, (NB, NB), 1)
    for i in range(BLOCKS):
        for j in range(i + 1):
            source = (i * col_devs + j % col_devs) * NB
            at = j // col_devs * NB
            block = d_ref[source : source + NB, at : at + NB].astype(jnp.float32)
            flipped = block.T
            if i == j:
                m_ref[i * NB : (i + 1) * NB, j * NB : (j + 1) * NB] = jnp.where(
                    r >= c, block, flipped
                )
            else:
                m_ref[i * NB : (i + 1) * NB, j * NB : (j + 1) * NB] = block
                m_ref[j * NB : (j + 1) * NB, i * NB : (i + 1) * NB] = flipped
    l_ref[...] = jnp.zeros_like(l_ref)

    def step(k, _):
        here = pl.ds(pl.multiple_of(k * NB, NB), NB)
        t_ref[:, :NB] = m_ref[here, here]
        t_ref[:, NB:] = jnp.where(r == c, 1.0, 0.0)
        factor_block(t_ref)
        l_ref[here, here] = t_ref[:, :NB].T
        inverse = t_ref[:, NB:]
        p_ref[...] = jnp.dot(
            inverse, m_ref[here, :], precision=HIGHEST, preferred_element_type=jnp.float32
        )
        p_ref[:, here] = inverse
        m_ref[here, :] = p_ref[...]

        def below(i, _):
            there = pl.ds(pl.multiple_of(i * NB, NB), NB)
            part = p_ref[:, there]
            l_ref[there, here] = part.T
            m_ref[there, here] = jnp.zeros((NB, NB), jnp.float32)
            m_ref[there, :] -= dot_tn(part, p_ref[...])
            return 0

        lax.fori_loop(k + 1, BLOCKS, below, 0)
        return 0

    lax.fori_loop(0, BLOCKS, step, 0)
    tall = lax.broadcasted_iota(jnp.int32, (WIDE, NB), 0)
    lane = lax.broadcasted_iota(jnp.int32, (WIDE, NB), 1)
    for j in range(BLOCKS):
        at = j // col_devs * NB
        inv_ref[j % col_devs, :, at : at + NB] = jnp.where(
            tall >= lane + j * NB, m_ref[:, j * NB : (j + 1) * NB], 0.0
        ).astype(jnp.bfloat16)


def factor_diagonal(corner, row_devs, col_devs):
    vmem = pl.BlockSpec(memory_space=pltpu.VMEM)
    return pl.pallas_call(
        functools.partial(factor_kernel, row_devs, col_devs),
        out_shape=(
            jax.ShapeDtypeStruct((WIDE, WIDE), jnp.float32),
            jax.ShapeDtypeStruct((col_devs, WIDE, WIDE // col_devs), jnp.bfloat16),
        ),
        in_specs=[vmem],
        out_specs=(vmem, vmem),
        scratch_shapes=[
            pltpu.VMEM((WIDE, WIDE), jnp.float32),
            pltpu.VMEM((NB, 2 * NB), jnp.float32),
            pltpu.VMEM((NB, WIDE), jnp.float32),
        ],
        compiler_params=pltpu.CompilerParams(vmem_limit_bytes=32 * 1024 * 1024),
        cost_estimate=pl.CostEstimate(
            flops=20 * WIDE**3, bytes_accessed=WIDE * WIDE * 8, transcendentals=WIDE
        ),
    )(corner)


def contract(a, b):
    return lax.dot_general(a, b, (((1,), (1,)), ((), ())), preferred_element_type=jnp.float32)


def solve_rows_kernel(*refs):
    count = len(refs) - 4
    raw = refs[:count]
    inv_ref, own_ref, out_ref, panel_ref = refs[count:]
    total = contract(raw[0][...], inv_ref[0])
    panel = contract(raw[0][...], own_ref[0])
    for d in range(1, count):
        total += contract(raw[d][...], inv_ref[d])
        panel += contract(raw[d][...], own_ref[d])
    out_ref[...] = total.astype(jnp.bfloat16)
    panel_ref[...] = panel


def solve_rows(pieces, inverse, own_inverse):
    rows, depth = pieces[0].shape
    height = 512
    vmem = pl.BlockSpec(memory_space=pltpu.VMEM)
    return pl.pallas_call(
        solve_rows_kernel,
        out_shape=(
            jax.ShapeDtypeStruct((rows, WIDE), jnp.bfloat16),
            jax.ShapeDtypeStruct((rows, depth), jnp.float32),
        ),
        grid=(rows // height,),
        in_specs=[pl.BlockSpec((height, depth), lambda g: (g, 0))] * len(pieces) + [vmem, vmem],
        out_specs=(
            pl.BlockSpec((height, WIDE), lambda g: (g, 0)),
            pl.BlockSpec((height, depth), lambda g: (g, 0)),
        ),
        compiler_params=pltpu.CompilerParams(vmem_limit_bytes=32 * 1024 * 1024),
        cost_estimate=pl.CostEstimate(
            flops=2 * rows * WIDE * (WIDE + depth), bytes_accessed=rows * WIDE * 4, transcendentals=0
        ),
    )(*pieces, inverse, own_inverse)


TALL = 4


def solve_cols_kernel(raw_ref, inv_ref, out_ref):
    count, depth = raw_ref.shape[0], raw_ref.shape[-1]
    total = None
    for q in range(count):
        term = contract(raw_ref[q, 0].reshape(TALL * NB, depth), inv_ref[q])
        total = term if total is None else total + term
    out_ref[...] = total.astype(jnp.bfloat16).reshape(TALL, 1, NB, WIDE)


def solve_cols(raw, inverse):
    col_devs, ratio, lrb, _, depth = raw.shape
    cols = ratio * lrb * NB
    out = pl.pallas_call(
        solve_cols_kernel,
        out_shape=jax.ShapeDtypeStruct((lrb, ratio, NB, WIDE), jnp.bfloat16),
        grid=(ratio, lrb // TALL),
        in_specs=[
            pl.BlockSpec((col_devs, 1, TALL, NB, depth), lambda o, g: (0, o, g, 0, 0)),
            pl.BlockSpec(memory_space=pltpu.VMEM),
        ],
        out_specs=pl.BlockSpec((TALL, 1, NB, WIDE), lambda o, g: (g, o, 0, 0)),
        compiler_params=pltpu.CompilerParams(vmem_limit_bytes=32 * 1024 * 1024),
        cost_estimate=pl.CostEstimate(
            flops=2 * cols * WIDE * WIDE, bytes_accessed=cols * WIDE * 4, transcendentals=0
        ),
    )(raw, inverse)
    return out.reshape(cols, WIDE)


STEP = 2
CHUNK = 4
STRIP = 8


def update_kernel(
    row_devs, col_devs, nc, own, ids, pos, front_ref, rowf_ref, colf_ref, panel_ref, tiles_ref, out_ref
):
    g = pl.program_id(0)
    row_here, col_here = pos[0], pos[1]
    r = lax.broadcasted_iota(jnp.int32, (NB, NB), 0)
    c = lax.broadcasted_iota(jnp.int32, (NB, NB), 1)

    def place(b, col):
        return pl.ds(b * NB * nc + col, NB, stride=nc)

    last_row = (g * STEP + STEP - 1) * row_devs + row_here
    linear = out_ref.reshape(STEP * NB, nc, NB)
    for chunk in range(0, nc, CHUNK):
        active = chunk * col_devs + col_here <= last_row
        strip = chunk // STRIP * STRIP
        strip_active = strip * col_devs + col_here <= last_row
        if chunk == strip:

            @pl.when(jnp.logical_not(strip_active))
            def _(strip=strip):
                linear[:, strip : strip + STRIP, :] = jnp.zeros((STEP * NB, STRIP, NB), jnp.float32)

        @pl.when(active)
        def _(chunk=chunk):
            product = lax.dot_general(
                rowf_ref[...],
                colf_ref[chunk * NB : (chunk + CHUNK) * NB, :],
                (((1,), (1,)), ((), ())),
                preferred_element_type=jnp.float32,
            )
            for b in range(STEP):
                row_block = (g * STEP + b) * row_devs + row_here
                for cc in range(CHUNK):
                    col = chunk + cc
                    if col < own:
                        out_ref[place(b, col), :] = panel_ref[
                            b * NB : (b + 1) * NB, col * NB : (col + 1) * NB
                        ]
                    else:
                        gap = (row_block - (col * col_devs + col_here)) * NB
                        value = (
                            front_ref[place(b, col), :]
                            - product[b * NB : (b + 1) * NB, cc * NB : (cc + 1) * NB]
                        )
                        out_ref[place(b, col), :] = jnp.where(r + gap >= c, value, 0.0)

        @pl.when(strip_active & jnp.logical_not(active))
        def _(chunk=chunk):
            for b in range(STEP):
                for cc in range(CHUNK):
                    out_ref[place(b, chunk + cc), :] = jnp.zeros((NB, NB), jnp.float32)

    def add_tile(t, _):
        block = ids[t]
        br = block // nc
        bc = block % nc

        @pl.when((br // STEP == g) & (bc >= own))
        def _():
            gap = (br * row_devs + row_here - (bc * col_devs + col_here)) * NB
            tile = tiles_ref[t].astype(jnp.float32)
            where = place(br % STEP, bc)
            out_ref[where, :] += jnp.where(r + gap >= c, tile, 0.0)

        return 0

    lax.fori_loop(0, tiles_ref.shape[0], add_tile, 0)


def update(front, rowf, colf, panel, tiles, ids, pos, row_devs, col_devs):
    rows, cols = rowf.shape[0], colf.shape[0]
    nc = cols // NB
    own = panel.shape[1] // NB
    height = STEP * NB
    return pl.pallas_call(
        functools.partial(update_kernel, row_devs, col_devs, nc, own),
        out_shape=jax.ShapeDtypeStruct((rows * nc, NB), jnp.float32),
        grid_spec=pltpu.PrefetchScalarGridSpec(
            num_scalar_prefetch=2,
            grid=(rows // height,),
            in_specs=[
                pl.BlockSpec((height * nc, NB), lambda g, *_: (g, 0)),
                pl.BlockSpec((height, WIDE), lambda g, *_: (g, 0)),
                pl.BlockSpec(memory_space=pltpu.VMEM),
                pl.BlockSpec((height, own * NB), lambda g, *_: (g, 0)),
                pl.BlockSpec(memory_space=pltpu.VMEM),
            ],
            out_specs=pl.BlockSpec((height * nc, NB), lambda g, *_: (g, 0)),
        ),
        compiler_params=pltpu.CompilerParams(vmem_limit_bytes=48 * 1024 * 1024),
        cost_estimate=pl.CostEstimate(
            flops=rows * cols * WIDE, bytes_accessed=rows * cols * 8, transcendentals=0
        ),
    )(ids, pos, front, rowf, colf, panel, tiles)


def place_tiles(tile_block, perm_block):
    width = tile_block.shape[-1]
    positions = jnp.arange(width, dtype=jnp.int32)
    row_onehot = (perm_block[:, 0, None, :] == positions[:, None]).astype(jnp.bfloat16)
    col_onehot = (perm_block[:, 1, None, :] == positions[:, None]).astype(jnp.bfloat16)
    moved = jnp.einsum(
        "axi,aij->axj", row_onehot, tile_block, preferred_element_type=jnp.float32
    ).astype(jnp.bfloat16)
    return jnp.einsum(
        "axj,ayj->axy", moved, col_onehot, preferred_element_type=jnp.float32
    ).astype(jnp.bfloat16)


def exchange(x):
    return lax.all_to_all(x, ("frow", "fcol"), split_axis=0, concat_axis=0, tiled=True)


def shards(front_orig, child_tiles, tile_target, tile_rows, tile_cols):
    row_devs = lax.axis_size("frow")
    col_devs = lax.axis_size("fcol")
    owners = row_devs * col_devs
    row_here = lax.axis_index("frow")
    col_here = lax.axis_index("fcol")
    held = child_tiles.shape[0]
    slot_count = owners * CAP
    owner_of = tile_target[:, 0]
    block_of = tile_target[:, 1]
    tile_order = jnp.arange(held, dtype=jnp.int32)
    same_owner = owner_of[:, None] == owner_of[None, :]
    earlier = tile_order[None, :] < tile_order[:, None]
    rank_of = jnp.sum(jnp.where(same_owner & earlier, 1, 0), axis=1).astype(jnp.int32)
    slot_of = owner_of * CAP + rank_of
    slot_match = slot_of[None, :] == jnp.arange(slot_count, dtype=jnp.int32)[:, None]
    source_tile = jnp.sum(jnp.where(slot_match, tile_order[None, :], 0), axis=1)
    lists = jnp.stack(
        [tile_rows, tile_cols, jnp.broadcast_to(block_of[:, None], tile_rows.shape)], axis=1
    )
    lists_in = exchange(jnp.take(lists, source_tile, axis=0).reshape(owners, CAP, 3, NB))
    tiles_in = exchange(jnp.take(child_tiles, source_tile, axis=0).reshape(owners, CAP, NB, NB))
    lists_in = lists_in.reshape(slot_count, 3, NB)
    ids = lists_in[:, 2, 0]
    placed = place_tiles(tiles_in.reshape(slot_count, NB, NB), lists_in[:, :2])

    rows, cols = front_orig.shape[1], front_orig.shape[3]
    lrb, nc = rows // NB, cols // NB
    own = BLOCKS // col_devs
    ratio = row_devs // col_devs

    panel_ids = (jnp.arange(lrb)[:, None] * nc + jnp.arange(own)[None, :]).reshape(-1, 1)
    panel_onehot = (ids[None, :] == panel_ids).astype(jnp.bfloat16)
    added = jnp.dot(
        panel_onehot, placed.reshape(slot_count, NB * NB), preferred_element_type=jnp.float32
    )
    added = added.reshape(lrb, own, NB, NB).transpose(0, 2, 1, 3).reshape(rows, own * NB)
    own_panel = (front_orig[0, :, 0, : own * NB] + added).astype(jnp.bfloat16)

    corner = lax.all_gather(own_panel[:NB], ("frow", "fcol"), axis=0, tiled=True)
    corner = corner[: BLOCKS * col_devs * NB]

    pieces = [own_panel]
    for shift in range(1, col_devs):
        route = [((q + shift) % col_devs, q) for q in range(col_devs)]
        pieces.append(lax.ppermute(own_panel, "fcol", route))
    route = []
    for p in range(row_devs):
        for q in range(col_devs):
            route.append((p * col_devs + q, (q * ratio + p // col_devs) * col_devs + p % col_devs))
    turned = lax.ppermute(own_panel, ("frow", "fcol"), route)
    col_raw = lax.all_gather(turned, "frow", axis=0, tiled=False)
    col_raw = col_raw.reshape(col_devs, ratio, lrb, NB, own * NB)

    lower, inverse = factor_diagonal(corner, row_devs, col_devs)

    turned_inverse = lax.dynamic_slice_in_dim(
        jnp.concatenate([inverse, inverse], axis=0), col_here, col_devs, axis=0
    )
    own_inverse = jnp.concatenate(
        [
            lax.dynamic_slice_in_dim(turned_inverse, (col_here + j * col_devs) * NB, NB, axis=1)
            for j in range(own)
        ],
        axis=1,
    )
    rowf, solved = solve_rows(pieces, turned_inverse, own_inverse)
    block = jnp.minimum(row_here, BLOCKS - 1)
    corner_own = jnp.concatenate(
        [
            lax.dynamic_slice(lower, (block * NB, (col_here + j * col_devs) * NB), (NB, NB))
            for j in range(own)
        ],
        axis=1,
    )
    panel = jnp.concatenate(
        [jnp.where(row_here < BLOCKS, corner_own, solved[:NB]), solved[NB:]], axis=0
    )
    colf = solve_cols(col_raw, inverse)

    out = update(
        front_orig.reshape(rows * nc, NB),
        rowf,
        colf,
        panel,
        placed,
        ids,
        jnp.stack([row_here, col_here]).astype(jnp.int32),
        row_devs,
        col_devs,
    )
    return out.reshape(front_orig.shape)


def solution(mesh):
    return jax.shard_map(
        shards,
        mesh=mesh,
        in_specs=(
            P("frow", None, "fcol", None),
            P(("frow", "fcol"), None, None),
            P(("frow", "fcol"), None),
            P(("frow", "fcol"), None),
            P(("frow", "fcol"), None),
        ),
        out_specs=P("frow", None, "fcol", None),
        check_vma=False,
    )
```
